32 devices in a mesh: grp: 4 (over x, core), dev: 8 (over z, y).
Axes of the slice: x: 2, y: 2, z: 4, core: 2. Of those that a mesh axis runs over, the one named last changes fastest.
Arguments:
- samples: bfloat16 [1024, 1024], P(('grp', 'dev')), may hold values from -0.1875 to 0.1875
- set_labels: int32 [1024], P(('grp', 'dev')), may hold values 0 or 1
- sign_words: int32 [1024, 25], P(('grp', 'dev')), may hold values from 0 to 2097151
- corpus: bfloat16 [1024, 1024], P(('grp', 'dev')), may hold values from -0.1875 to 0.1875
- scale_grid: float32 [16], replicated, may hold values from 0.25 to 4
- scale_pick: int32 [4], replicated, may hold values from 0 to 15
Outputs:
- quad_forms: float32 [4, 512], replicated
- test_scores: float32 [4], replicated
- proof: float32 [4, 1024], P(None, ('grp', 'dev'))
The draws below stay inside these ranges and needn't reach their ends.
Inputs may be any that keep to these rules, and one draw needn't show every extreme that they name: `sign_words`: every word is below 2 ** 21; each of its 21 bits is a sign, 1 for +1 and 0 for -1. `scale_pick`: indices into the grid, from 0 to 15.
All inputs are finite; a program needn't handle non-finite values. No bound on the sum of `set_labels` on one device may be relied on, other than what follows from the above.
Results may differ from the reference program's by a relative error of at most 0.0099.
Values may be sent and summed in bfloat16 or wider, within the bound.
A program may use at most 64 MiB of HBM per device.

```python
import math
import jax
import jax.numpy as jnp
from jax import lax

D = 1024
NB = 4
GRID = 16
BOOT = 511
WORDS = 25
M = 1024
CORPUS = 1024
N_GRP = 4


def set_ends(result, rng, least, top_value):
    longest = result.shape.index(max(result.shape))
    spots = []
    for shift in (0, 1):
        where = [jax.random.randint(jax.random.fold_in(rng, axis), (), 0, length) for axis, length in enumerate(result.shape)]
        where[longest] = (where[longest] + shift) % result.shape[longest]
        spots.append(tuple(where))
    return result.at[spots[0]].set(least).at[spots[1]].set(top_value)


def level_of(key, dims, split, smallest, top_value):
    gain, own = 1.0, jax.random.fold_in(key, 6)
    for axis_at, shards_of in split:
        heights = jnp.exp(jax.random.uniform(jax.random.fold_in(own, axis_at), (shards_of,), jnp.float32, smallest / len(split), top_value / len(split)))
        gain = gain * jnp.repeat(heights, dims[axis_at] // shards_of).reshape([-1 if axis == axis_at else 1 for axis in range(len(dims))])
    return gain


def scatter_about(own_key, shape, scale, reach, cuts=(), kind=jnp.bfloat16):
    result = scale * jax.random.normal(own_key, shape, jnp.float32)
    if cuts:
        result = result * level_of(own_key, shape, cuts, -0.22, 0.18)
    return jnp.clip(result, -reach, reach).astype(kind)


def setup_inputs(seed: int = 0) -> dict:
    keys = jax.random.split(jax.random.key(seed), 7)
    samples = scatter_about(keys[0], (M, D), (D ** -0.5), 0.1875, ((0, 32),))
    set_labels = set_ends((jax.random.randint(keys[1], (M,), 0, 2) < 1).astype(jnp.int32), jax.random.fold_in(keys[1], 1), 0, 1)
    sign_words = set_ends(jax.random.randint(keys[2], (M, WORDS), 0, 2097152), jax.random.fold_in(keys[2], 1), 0, 2097151).astype(jnp.int32)
    corpus = scatter_about(keys[3], (CORPUS, D), (D ** -0.5), 0.1875, ((0, 32),))
    scale_grid = jnp.clip(jnp.exp(jax.random.uniform(keys[4], (GRID,), jnp.float32, math.log(0.25), math.log(4.0))), 0.25, 4.0)
    scale_pick = set_ends(jax.random.randint(keys[5], (NB,), 0, GRID), jax.random.fold_in(keys[5], 1), 0, GRID - 1).astype(jnp.int32)
    return dict(samples=samples, set_labels=set_labels, sign_words=sign_words, corpus=corpus, scale_grid=scale_grid, scale_pick=scale_pick)


word_bits = 21

def make_vectors(set_labels, sign_words):
    weights = (1 - 2 * set_labels).astype(jnp.float32)
    shifts = jnp.arange(word_bits, dtype=jnp.int32)
    bit_flags = jnp.right_shift(sign_words[:, :, None], shifts[None, None, :]) & 1
    bit_flags = bit_flags.reshape(sign_words.shape[0], -1)[:, :BOOT]
    sign_values = (2 * bit_flags - 1).astype(jnp.float32)
    vectors = jnp.concatenate([weights[:, None], sign_values * weights[:, None]], axis=1)
    return vectors.astype(jnp.bfloat16)

def band_scales(scale_grid, scale_pick):
    onehot = (scale_pick[:, None] == jnp.arange(scale_grid.shape[0], dtype=jnp.int32)[None, :]).astype(jnp.float32)
    chosen = lax.optimization_barrier(jnp.sum(onehot * scale_grid[None, :], axis=1))
    return 0.5 / chosen

def rounded(values):
    narrow = values.astype(jnp.bfloat16)
    narrow = lax.optimization_barrier(narrow)
    return narrow.astype(jnp.float32)

def reference(samples, set_labels, sign_words, corpus, scale_grid, scale_pick):
    vectors = make_vectors(set_labels, sign_words).astype(jnp.float32)
    scales = band_scales(scale_grid, scale_pick)
    samples_wide = samples.astype(jnp.float32)
    corpus_wide = corpus.astype(jnp.float32)
    sample_sq = lax.optimization_barrier(jnp.sum(samples_wide * samples_wide, axis=1))
    corpus_sq = lax.optimization_barrier(jnp.sum(corpus_wide * corpus_wide, axis=1))
    total = samples.shape[0]
    span = total // N_GRP
    corpus_span = corpus.shape[0] // N_GRP
    weights = vectors[:, 0]

    def test_block(block_id):
        offset = (block_id * span).astype(jnp.int32)
        block_rows = lax.dynamic_slice_in_dim(samples_wide, offset, span, 0)
        block_sq = lax.dynamic_slice_in_dim(sample_sq, offset, span, 0)
        block_vec = lax.dynamic_slice_in_dim(vectors, offset, span, 0)
        cross = jnp.dot(block_rows, samples_wide.T, precision=lax.Precision.HIGHEST)
        dist = block_sq[:, None] + sample_sq[None, :] - 2.0 * cross
        results = []
        for kernel_id in range(NB):
            kern = rounded(jnp.exp(-dist * scales[kernel_id]))
            product = jnp.dot(kern, vectors, precision=lax.Precision.HIGHEST)
            results.append(lax.optimization_barrier(jnp.sum(block_vec * product, axis=0)))
        return jnp.stack(results)
    partial_forms = lax.map(test_block, jnp.arange(N_GRP, dtype=jnp.int32))
    quad_forms = lax.optimization_barrier(jnp.sum(partial_forms, axis=0)) / total
    bootstrap = quad_forms[:, 1:]
    centre = lax.optimization_barrier(jnp.mean(bootstrap, axis=1))
    spread = lax.optimization_barrier(jnp.mean(jnp.square(bootstrap - centre[:, None]), axis=1))
    test_scores = (quad_forms[:, 0] - centre) / jnp.sqrt(spread + 1e-06)

    def proof_block(block_id):
        offset = (block_id * corpus_span).astype(jnp.int32)
        block_rows = lax.dynamic_slice_in_dim(corpus_wide, offset, corpus_span, 0)
        block_sq = lax.dynamic_slice_in_dim(corpus_sq, offset, corpus_span, 0)
        cross = jnp.dot(block_rows, samples_wide.T, precision=lax.Precision.HIGHEST)
        dist = block_sq[:, None] + sample_sq[None, :] - 2.0 * cross
        results = []
        for kernel_id in range(NB):
            kern = rounded(jnp.exp(-dist * scales[kernel_id]))
            results.append(jnp.dot(kern, weights, precision=lax.Precision.HIGHEST))
        return jnp.stack(results)
    proof_parts = lax.map(proof_block, jnp.arange(N_GRP, dtype=jnp.int32))
    proof = jnp.transpose(proof_parts, (1, 0, 2)).reshape(NB, corpus.shape[0])
    inv_root = jnp.float32(1.0) / jnp.sqrt(jnp.float32(total))
    proof = proof * inv_root
    return (quad_forms, test_scores, proof)
```

```python
import functools
import math

import jax
import jax.numpy as jnp
from jax import lax
from jax.experimental import pallas as pl
from jax.experimental.pallas import tpu as pltpu
from jax.sharding import PartitionSpec as P

WORD_BITS = 21
CORES = 2
LOG2E = math.log2(math.e)
MESH = pl.DeviceIdType.MESH
F32 = jnp.float32
BF16 = jnp.bfloat16


def loop(count, body):
    if count == 1:
        body(0)
    else:
        lax.fori_loop(0, count, lambda i, c: (body(i), c)[1], 0)


def aligned(index, size):
    return index * size if isinstance(index, int) else pl.multiple_of(index * size, size)


def kernel(geo, samples, labels, words, corpus, grid, pick, quad_out, score_out, proof_out,
           row_s, row_c, col_s, word_in, label_in, row_pack, col_pack, row_vec, col_vec,
           part1, part2, local_sem, rp_send, rp_recv, cp_send, cp_recv, rs_send, rs_recv,
           rc_send, rc_recv, cs_send, cs_recv, fw_send, fw_recv, p1_send, p1_recv, p2_send, p2_recv):
    n_gx, n_lo, n_hi = geo
    own = samples.shape[0]
    n_bands, n_vec = quad_out.shape
    n_row, n_col, n_plane = n_gx * n_lo, n_hi * CORES, n_gx * n_lo * CORES
    rows, cols = n_row * own, n_col * own
    n_words = words.shape[1]
    total = n_row * n_col * own

    grp, dev = lax.axis_index("grp"), lax.axis_index("dev")
    gx, core = grp // CORES, grp % CORES
    z, lo = dev // n_lo, dev % n_lo
    other = 1 - core
    rslot = gx * n_lo + lo
    cslot = z * CORES + core
    pslot = rslot * CORES + core

    def at_row(slot, core_):
        return ((slot // n_lo) * CORES + core_, z * n_lo + slot % n_lo)

    def at_col(z_, core_):
        return (gx * CORES + core_, z_ * n_lo + lo)

    barrier = pltpu.get_barrier_semaphore()
    partners = []
    for t in range(1, n_plane):
        slot = (pslot + t) % n_plane
        partners.append(at_row(slot // CORES, slot % CORES))
    for t in range(1, n_hi):
        partners.append(at_col((z + t) % n_hi, core))
        partners.append(at_col((z + t) % n_hi, other))

    word_copy = pltpu.make_async_copy(words, word_in, local_sem.at[0])
    label_copy = pltpu.make_async_copy(labels, label_in, local_sem.at[1])
    word_copy.start()
    label_copy.start()
    for p in partners:
        pl.semaphore_signal(barrier, inc=1, device_id=p, device_id_type=MESH)
    own_rows = pl.ds(pl.multiple_of(rslot * own, own), own)
    own_cols = pl.ds(pl.multiple_of(cslot * own, own), own)
    keep = [
        pltpu.make_async_copy(samples, row_s.at[own_rows], local_sem.at[2]),
        pltpu.make_async_copy(corpus, row_c.at[own_rows], local_sem.at[3]),
        pltpu.make_async_copy(samples, col_s.at[own_cols], local_sem.at[4]),
    ]
    for c in keep:
        c.start()

    pl.semaphore_wait(barrier, len(partners))

    def remote(src, dst, send, recv, to):
        return pltpu.make_async_remote_copy(
            src_ref=src, dst_ref=dst, send_sem=send, recv_sem=recv, device_id=to, device_id_type=MESH)

    sends = []
    col_in, fw_in, rs_in, rc_in = [], [], [], []

    def col_block(slot):
        return col_s.at[pl.ds(pl.multiple_of(slot * own, own), own)]

    def row_block(ref, slot):
        return ref.at[pl.ds(pl.multiple_of(slot * own, own), own)]

    for t in range(1, n_hi):
        to = (z + t) % n_hi
        c = remote(samples, col_block(cslot), cs_send.at[t], cs_recv.at[z], at_col(to, core))
        c.start()
        sends.append(c)
    for t in range(1, n_row):
        to = (rslot + t) % n_row
        c = remote(samples, row_block(row_s, rslot), rs_send.at[t], rs_recv.at[rslot], at_row(to, core))
        c.start()
        sends.append(c)
    c = remote(samples, col_block(cslot), fw_send.at[z], fw_recv.at[z], at_col(z, other))
    c.start()
    sends.append(c)

    word_copy.wait()
    label_copy.wait()
    eye = lax.broadcasted_iota(jnp.int32, (own, own), 0) == lax.broadcasted_iota(jnp.int32, (own, own), 1)
    label_col = jnp.sum(jnp.where(eye, label_in[...].astype(F32), 0.0), axis=1, keepdims=True).astype(jnp.int32)
    groups = own // 8
    pieces = []
    width = 128 // groups
    for q in range(groups):
        pieces.append(word_in[pl.ds(8 * q, 8), :])
        pieces.append(label_col[8 * q:8 * q + 8])
        pieces.append(jnp.zeros((8, width - n_words - 1), jnp.int32))
    packed = jnp.concatenate(pieces, axis=1)
    col_pack[cslot] = packed
    row_pack[rslot] = packed

    for t in range(1, n_col):
        to = (cslot + t) % n_col
        c = remote(col_pack.at[cslot], col_pack.at[cslot], cp_send.at[t], cp_recv.at[cslot],
                   at_col(to // CORES, to % CORES))
        c.start()
        sends.append(c)
    for t in range(1, n_row):
        to = (rslot + t) % n_row
        c = remote(row_pack.at[rslot], row_pack.at[rslot], rp_send.at[t], rp_recv.at[rslot], at_row(to, core))
        c.start()
        sends.append(c)
    for t in range(1, n_row):
        to = (rslot + t) % n_row
        c = remote(corpus, row_block(row_c, rslot), rc_send.at[t], rc_recv.at[rslot], at_row(to, core))
        c.start()
        sends.append(c)

    for t in range(1, n_hi):
        src = (z + n_hi - t) % n_hi
        block = col_block(src * CORES + core)
        remote(samples, block, cs_send.at[t], cs_recv.at[src], at_col(src, core)).wait_recv()
        c = remote(block, block, fw_send.at[src], fw_recv.at[src], at_col(z, other))
        c.start()
        sends.append(c)

    lane = lax.broadcasted_iota(jnp.int32, (8, 128), 1)
    label_lane = lane - lane % width + n_words
    is_label = lane % width == n_words
    n_chunks = n_vec // 128
    index, mask = [], []
    for t in range(n_chunks):
        k = jnp.maximum(lane + (128 * t - 1), 0)
        w = (k * 3121) >> 16
        shift = k - w * WORD_BITS
        if t == 0:
            w = jnp.where(lane == 0, n_words, w)
            shift = jnp.where(lane == 0, 0, shift)
        index.append(w)
        mask.append(jnp.int32(1) << shift)

    def expand(tile, dst, base):
        label = jnp.take_along_axis(tile, label_lane, axis=1)
        tile = jnp.where(is_label, label ^ 1, tile ^ (0 - label))
        for t in range(n_chunks):
            parts = []
            for q in range(groups):
                got = jnp.take_along_axis(tile, index[t] + q * width, axis=1)
                parts.append(jnp.where((got & mask[t]) != 0, 1.0, -1.0).astype(F32))
            dst[pl.ds(base, own), pl.ds(128 * t, 128)] = jnp.concatenate(parts, axis=0).astype(dst.dtype)

    for t in range(1, n_col):
        src = (cslot + n_col - t) % n_col
        remote(col_pack.at[src], col_pack.at[src], cp_send.at[t], cp_recv.at[src],
               at_col(src // CORES, src % CORES)).wait_recv()
    for t in range(1, n_row):
        src = (rslot + n_row - t) % n_row
        remote(row_pack.at[src], row_pack.at[src], rp_send.at[t], rp_recv.at[src], at_row(src, core)).wait_recv()
    for slot in range(n_col):
        expand(col_pack[slot], col_vec, slot * own)
    for slot in range(n_row):
        expand(row_pack[slot], row_vec, slot * own)

    for c in keep:
        c.wait()
    for t in range(n_hi):
        src = (z + n_hi - t) % n_hi
        block = col_block(src * CORES + other)
        remote(samples, block, fw_send.at[src], fw_recv.at[src], at_col(z, other)).wait_recv()
    for t in range(1, n_row):
        src = (rslot + n_row - t) % n_row
        remote(samples, row_block(row_s, src), rs_send.at[t], rs_recv.at[src], at_row(src, core)).wait_recv()
    for t in range(1, n_row):
        src = (rslot + n_row - t) % n_row
        remote(corpus, row_block(row_c, src), rc_send.at[t], rc_recv.at[src], at_row(src, core)).wait_recv()

    rb, cb = min(128, rows), min(256, cols)
    gains = [jnp.full((1, 1), -0.5 * LOG2E, F32) / jnp.full((1, 1), grid[pick[b]], F32) for b in range(n_bands)]
    diag = lax.broadcasted_iota(jnp.int32, (cb, cb), 0) == lax.broadcasted_iota(jnp.int32, (cb, cb), 1)
    if rows > rb or cols > cb:
        part1[pslot] = jnp.zeros(part1.shape[1:], F32)

    def squares(x):
        wide = x.astype(F32)
        return jnp.sum(wide * wide, axis=1, keepdims=True)

    def kerns(left, right, right_sq):
        cross = lax.dot_general(left, right, (((1,), (1,)), ((), ())), preferred_element_type=F32)
        dist = squares(left) + right_sq - 2.0 * cross
        return jnp.concatenate([jnp.exp2(dist * g).astype(BF16) for g in gains], axis=0)

    def add_to(lanes, value):
        if rows > rb or cols > cb:
            value = part1[pslot, :, lanes] + value
        part1[pslot, :, lanes] = value

    def column_chunk(cc):
        here = pl.ds(aligned(cc, cb), cb)
        right = col_s[here, :]
        right_sq = jnp.sum(jnp.where(diag, squares(right), 0.0), axis=0, keepdims=True)
        vec = col_vec[here, :]

        def row_chunk(rc):
            there = pl.ds(aligned(rc, rb), rb)
            kern = kerns(row_s[there, :], right, right_sq)
            prod = jnp.dot(kern, vec, preferred_element_type=F32)
            mine = row_vec[there, :]
            forms = [jnp.sum(mine * prod[b * rb:(b + 1) * rb], axis=0, keepdims=True) for b in range(n_bands)]
            add_to(pl.ds(0, n_vec), jnp.concatenate(forms, axis=0))
            kern = kerns(row_c[there, :], right, right_sq)
            flat = lax.dot_general(vec[:, :128], kern, (((0,), (1,)), ((), ())), preferred_element_type=F32)
            proof = jnp.concatenate([flat[0:1, b * rb:(b + 1) * rb] for b in range(n_bands)], axis=0)
            add_to(pl.ds(aligned(rc, rb) + n_vec, rb), proof)

        loop(rows // rb, row_chunk)

    loop(cols // cb, column_chunk)

    for t in range(1, n_plane):
        to = (pslot + t) % n_plane
        c = remote(part1.at[pslot], part1.at[pslot], p1_send.at[t], p1_recv.at[pslot],
                   at_row(to // CORES, to % CORES))
        c.start()
        sends.append(c)
    for t in range(1, n_plane):
        src = (pslot + n_plane - t) % n_plane
        remote(part1.at[src], part1.at[src], p1_send.at[t], p1_recv.at[src],
               at_row(src // CORES, src % CORES)).wait_recv()
    quad = part1[0, :, :n_vec]
    for slot in range(1, n_plane):
        quad = quad + part1[slot, :, :n_vec]
    part2[z] = quad
    for t in range(1, n_hi):
        to = (z + t) % n_hi
        c = remote(part2.at[z], part2.at[z], p2_send.at[t], p2_recv.at[z], at_col(to, core))
        c.start()
        sends.append(c)
    proof = part1[core, :, n_vec:]
    for slot in range(1, n_row):
        proof = proof + part1[slot * CORES + core, :, n_vec:]
    mine = jnp.zeros((n_bands, own), F32)
    for slot in range(n_row):
        mine = jnp.where(rslot == slot, proof[:, slot * own:(slot + 1) * own], mine)
    proof_out[...] = mine * F32(1.0 / math.sqrt(total))
    for t in range(1, n_hi):
        src = (z + n_hi - t) % n_hi
        remote(part2.at[src], part2.at[src], p2_send.at[t], p2_recv.at[src], at_col(src, core)).wait_recv()
    quad = part2[0]
    for slot in range(1, n_hi):
        quad = quad + part2[slot]
    quad = quad * F32(1.0 / total)
    quad_out[...] = quad
    boot = lax.broadcasted_iota(jnp.int32, quad.shape, 1) > 0
    count = F32(1.0 / (n_vec - 1))
    centre = jnp.sum(jnp.where(boot, quad, 0.0), axis=1, keepdims=True) * count
    off = quad - centre
    spread = jnp.sum(jnp.where(boot, off * off, 0.0), axis=1, keepdims=True) * count
    score = (quad[:, :1] - centre) / jnp.sqrt(spread + 1e-6)
    spot = lax.broadcasted_iota(jnp.int32, (n_bands, n_bands), 0) == lax.broadcasted_iota(
        jnp.int32, (n_bands, n_bands), 1)
    score_out[...] = jnp.sum(jnp.where(spot, score, 0.0), axis=0, keepdims=True)
    for c in sends:
        c.wait_send()


def per_device(n_grp, n_dev, samples, labels, words, corpus, grid, pick):
    n_lo = 2 if n_dev % 2 == 0 else 1
    n_gx, n_hi = n_grp // CORES, n_dev // n_lo
    n_row, n_col, n_plane = n_gx * n_lo, n_hi * CORES, n_gx * n_lo * CORES
    own, width = samples.shape
    rows, cols = n_row * own, n_col * own
    n_bands, n_vec = pick.shape[0], 512
    dma = lambda n: pltpu.SemaphoreType.DMA((n,))
    any_ = pl.BlockSpec(memory_space=pl.ANY)
    vmem = pl.BlockSpec(memory_space=pltpu.VMEM)
    smem = pl.BlockSpec(memory_space=pltpu.SMEM)
    quad, score, proof = pl.pallas_call(
        functools.partial(kernel, (n_gx, n_lo, n_hi)),
        out_shape=(
            jax.ShapeDtypeStruct((n_bands, n_vec), F32),
            jax.ShapeDtypeStruct((1, n_bands), F32),
            jax.ShapeDtypeStruct((n_bands, own), F32),
        ),
        in_specs=[any_, any_, any_, any_, smem, smem],
        out_specs=(vmem, vmem, vmem),
        scratch_shapes=[
            pltpu.VMEM((rows, width), BF16),
            pltpu.VMEM((rows, width), BF16),
            pltpu.VMEM((cols, width), BF16),
            pltpu.VMEM(words.shape, jnp.int32),
            pltpu.VMEM((1, own), jnp.int32),
            pltpu.VMEM((n_row, 8, 128), jnp.int32),
            pltpu.VMEM((n_col, 8, 128), jnp.int32),
            pltpu.VMEM((rows, n_vec), F32),
            pltpu.VMEM((cols, n_vec), BF16),
            pltpu.VMEM((n_plane, n_bands, n_vec + rows), F32),
            pltpu.VMEM((n_hi, n_bands, n_vec), F32),
            dma(5),
            dma(n_row), dma(n_row), dma(n_col), dma(n_col), dma(n_row), dma(n_row),
            dma(n_row), dma(n_row), dma(n_hi), dma(n_hi), dma(n_hi), dma(n_hi),
            dma(n_plane), dma(n_plane), dma(n_hi), dma(n_hi),
        ],
        compiler_params=pltpu.CompilerParams(
            collective_id=0, has_side_effects=True, vmem_limit_bytes=48 * 1024 * 1024),
        name="two_sample",
    )(samples, labels.reshape(1, own), words, corpus, grid, pick)
    return quad, score.reshape(n_bands), proof


def solution(mesh):
    in_specs = (
        P(("grp", "dev"), None),
        P(("grp", "dev")),
        P(("grp", "dev"), None),
        P(("grp", "dev"), None),
        P(),
        P(),
    )
    out_specs = (P(), P(), P(None, ("grp", "dev")))
    return jax.shard_map(
        functools.partial(per_device, mesh.shape["grp"], mesh.shape["dev"]),
        mesh=mesh, in_specs=in_specs, out_specs=out_specs, check_vma=False
    )
```

```python
import functools
import math

import jax
import jax.numpy as jnp
from jax import lax
from jax.experimental import pallas as pl
from jax.experimental.pallas import tpu as pltpu
from jax.sharding import PartitionSpec as P

WORD_BITS = 21
CORES = 2
LOG2E = math.log2(math.e)
MESH = pl.DeviceIdType.MESH
F32 = jnp.float32
BF16 = jnp.bfloat16


def loop(count, body):
    if count == 1:
        body(0)
    else:
        lax.fori_loop(0, count, lambda i, c: (body(i), c)[1], 0)


def aligned(index, size):
    return index * size if isinstance(index, int) else pl.multiple_of(index * size, size)


def kernel(geo, samples, labels, words, corpus, grid, pick, quad_out, score_out, proof_out,
           row_s, row_c, col_s, word_in, label_in, grid_in, pick_in, row_pack, col_pack, row_vec, col_vec,
           part1, part2, pair_sem, local_sem, rp_send, rp_recv, rs_send, rs_recv, rc_send, rc_recv,
           cp_send, cp_recv, cs_send, cs_recv, fp_send, fp_recv, fw_send, fw_recv,
           p1_send, p1_recv, p2_send, p2_recv):
    n_gx, n_lo, n_hi = geo
    own = samples.shape[0]
    n_bands, n_vec = quad_out.shape
    n_row, n_col, n_plane = n_gx * n_lo, n_hi * CORES, n_gx * n_lo * CORES
    rows, cols = n_row * own, n_col * own
    n_words = words.shape[1]
    total = n_row * n_col * own

    grp, dev = lax.axis_index("grp"), lax.axis_index("dev")
    gx, core = grp // CORES, grp % CORES
    z, lo = dev // n_lo, dev % n_lo
    other = 1 - core
    rslot = gx * n_lo + lo
    cslot = z * CORES + core
    pslot = rslot * CORES + core

    def at_row(slot, core_):
        return ((slot // n_lo) * CORES + core_, z * n_lo + slot % n_lo)

    def at_col(z_, core_):
        return (gx * CORES + core_, z_ * n_lo + lo)

    barrier = pltpu.get_barrier_semaphore()
    up, down = z < n_hi - 1, z > 0
    partners = [at_col(z, other)]
    for t in range(1, n_gx):
        partners.append(at_row((gx + t) % n_gx * n_lo + lo, core))
    for t in range(1, n_lo):
        partners.append(at_row(gx * n_lo + (lo + t) % n_lo, core))

    def greet(to):
        pl.semaphore_signal(barrier, inc=1, device_id=to, device_id_type=MESH)

    word_copy = pltpu.make_async_copy(words, word_in, local_sem.at[0])
    label_copy = pltpu.make_async_copy(labels, label_in, local_sem.at[1])
    word_copy.start()
    label_copy.start()
    for p in partners:
        greet(p)
    pl.when(up)(lambda: greet(at_col(z + 1, core)))
    pl.when(down)(lambda: greet(at_col(z - 1, core)))
    own_rows = pl.ds(pl.multiple_of(rslot * own, own), own)
    own_cols = pl.ds(pl.multiple_of(cslot * own, own), own)
    keep = [
        pltpu.make_async_copy(samples, row_s.at[own_rows], local_sem.at[2]),
        pltpu.make_async_copy(corpus, row_c.at[own_rows], local_sem.at[3]),
        pltpu.make_async_copy(samples, col_s.at[own_cols], local_sem.at[4]),
        pltpu.make_async_copy(grid, grid_in, local_sem.at[5]),
        pltpu.make_async_copy(pick, pick_in, local_sem.at[6]),
    ]
    for c in keep:
        c.start()

    def remote(src, dst, send, recv, to):
        return pltpu.make_async_remote_copy(
            src_ref=src, dst_ref=dst, send_sem=send, recv_sem=recv, device_id=to, device_id_type=MESH)

    sends, cond_sends = [], []

    def go(c):
        c.start()
        sends.append(c)

    def go_if(cond, c):
        pl.when(cond)(c.start)
        cond_sends.append((cond, c))

    def block(ref, slot):
        return ref.at[pl.ds(pl.multiple_of(slot * own, own), own)]

    word_copy.wait()
    label_copy.wait()
    eye = lax.broadcasted_iota(jnp.int32, (own, own), 0) == lax.broadcasted_iota(jnp.int32, (own, own), 1)
    label_col = jnp.sum(jnp.where(eye, label_in[...].astype(F32), 0.0), axis=1, keepdims=True).astype(jnp.int32)
    groups = own // 8
    pieces = []
    width = 128 // groups
    for q in range(groups):
        pieces.append(word_in[pl.ds(8 * q, 8), :])
        pieces.append(label_col[8 * q:8 * q + 8])
        pieces.append(jnp.zeros((8, width - n_words - 1), jnp.int32))
    packed = jnp.concatenate(pieces, axis=1)
    col_pack[cslot] = packed
    row_pack[rslot] = packed

    pl.semaphore_wait(barrier, len(partners) + up.astype(jnp.int32) + down.astype(jnp.int32))

    def hop(tile, src, step, to_z, way):
        if tile:
            ref = col_pack.at[src * CORES + core]
            return remote(ref, ref, cp_send.at[way, step], cp_recv.at[src], at_col(to_z, core))
        ref = block(col_s, src * CORES + core)
        return remote(samples if step == 0 else ref, ref, cs_send.at[way, step], cs_recv.at[src], at_col(to_z, core))

    def side(tile, src):
        if tile:
            ref = col_pack.at[src * CORES + core]
            return remote(ref, ref, fp_send.at[src], fp_recv.at[src], at_col(z, other))
        ref = block(col_s, src * CORES + core)
        return remote(ref, ref, fw_send.at[src], fw_recv.at[src], at_col(z, other))

    def row_hop(which, slot, to, mine=False):
        ref, send, recv = {"p": (row_pack, rp_send, rp_recv), "s": (row_s, rs_send, rs_recv),
                           "c": (row_c, rc_send, rc_recv)}[which]
        if which == "p":
            dst = ref.at[slot]
            src = dst
        else:
            dst = block(ref, slot)
            src = {"s": samples, "c": corpus}[which] if mine else dst
        return remote(src, dst, send.at[slot, to], recv.at[slot], at_row(to, core))

    def xs(slot):
        return [(slot // n_lo + t) % n_gx * n_lo + slot % n_lo for t in range(1, n_gx)]

    def ys(slot):
        return [slot // n_lo * n_lo + (slot % n_lo + t) % n_lo for t in range(1, n_lo)]

    for tile in (True, False):
        go_if(down, hop(tile, z, 0, z - 1, 0))
        go_if(up, hop(tile, z, 0, z + 1, 1))
        for which in ("p",) if tile else ("s", "c"):
            for to in xs(rslot) + ys(rslot):
                go(row_hop(which, rslot, to, mine=True))
        if tile:
            go(side(True, z))
    go(remote(samples, block(col_s, cslot), fw_send.at[z], fw_recv.at[z], at_col(z, other)))

    def chain(tile, way):
        for d in range(1, n_hi):
            src = z - d if way == 1 else z + d
            here = src >= 0 if way == 1 else src < n_hi
            onward = here & (up if way == 1 else down)
            src = jnp.clip(src, 0, n_hi - 1)
            nxt = jnp.clip(z + 1 if way == 1 else z - 1, 0, n_hi - 1)
            step = min(d, n_hi - 2)
            c = hop(tile, src, step, nxt, 1 if way == 1 else 0)
            f = side(tile, src)

            @pl.when(here)
            def _():
                c.wait_recv()
                f.start()

            if d < n_hi - 1:
                pl.when(onward)(c.start)
                cond_sends.append((onward, c))
            cond_sends.append((here, f))

    def turn(which):
        first, then = (ys, xs) if which == "c" else (xs, ys)
        for src in first(rslot):
            row_hop(which, src, rslot).wait_recv()
            for to in then(rslot):
                go(row_hop(which, src, to))

    turn("p")
    chain(True, 1)
    turn("s")
    turn("c")
    chain(False, 1)
    chain(True, 0)
    chain(False, 0)

    lane = lax.broadcasted_iota(jnp.int32, (8, 128), 1)
    label_lane = lane - lane % width + n_words
    is_label = lane % width == n_words
    n_chunks = n_vec // 128
    index, mask = [], []
    for t in range(n_chunks):
        k = jnp.maximum(lane + (128 * t - 1), 0)
        w = (k * 3121) >> 16
        shift = k - w * WORD_BITS
        if t == 0:
            w = jnp.where(lane == 0, n_words, w)
            shift = jnp.where(lane == 0, 0, shift)
        index.append(w)
        mask.append(jnp.int32(1) << shift)

    def expand(tile, dst, base):
        label = jnp.take_along_axis(tile, label_lane, axis=1)
        tile = jnp.where(is_label, label ^ 1, tile ^ (0 - label))
        for t in range(n_chunks):
            parts = []
            for q in range(groups):
                got = jnp.take_along_axis(tile, index[t] + q * width, axis=1)
                parts.append(jnp.where((got & mask[t]) != 0, 1.0, -1.0).astype(F32))
            dst[pl.ds(base, own), pl.ds(128 * t, 128)] = jnp.concatenate(parts, axis=0).astype(dst.dtype)

    def late(which):
        first, then = (ys, xs) if which == "c" else (xs, ys)
        for src in then(rslot):
            row_hop(which, src, rslot).wait_recv()
            for far in first(src):
                row_hop(which, far, rslot).wait_recv()

    late("p")
    for t in range(n_hi):
        src = (z + t) % n_hi
        ref = col_pack.at[src * CORES + other]
        remote(ref, ref, fp_send.at[src], fp_recv.at[src], at_col(z, other)).wait_recv()
    for slot in range(n_col):
        expand(col_pack[slot], col_vec, slot * own)
    for slot in range(n_row):
        expand(row_pack[slot], row_vec, slot * own)

    for c in keep:
        c.wait()
    late("s")
    late("c")
    pl.semaphore_signal(pair_sem, inc=1, device_id=at_col(z, other), device_id_type=MESH)
    for t in range(n_hi):
        src = (z + t) % n_hi
        ref = block(col_s, src * CORES + other)
        remote(ref, ref, fw_send.at[src], fw_recv.at[src], at_col(z, other)).wait_recv()

    rb, cb = min(128, rows), min(256, cols)
    gains = [jnp.full((1, 1), -0.5 * LOG2E, F32) / jnp.full((1, 1), grid_in[pick_in[b]], F32) for b in range(n_bands)]
    diag = lax.broadcasted_iota(jnp.int32, (cb, cb), 0) == lax.broadcasted_iota(jnp.int32, (cb, cb), 1)
    if rows > rb or cols > cb:
        part1[pslot] = jnp.zeros(part1.shape[1:], F32)

    def squares(x):
        wide = x.astype(F32)
        return jnp.sum(wide * wide, axis=1, keepdims=True)

    def kerns(left, right, right_sq):
        cross = lax.dot_general(left, right, (((1,), (1,)), ((), ())), preferred_element_type=F32)
        dist = squares(left) + right_sq - 2.0 * cross
        return jnp.concatenate([jnp.exp2(dist * g).astype(BF16) for g in gains], axis=0)

    def add_to(lanes, value):
        if rows > rb or cols > cb:
            value = part1[pslot, :, lanes] + value
        part1[pslot, :, lanes] = value

    def column_chunk(cc):
        here = pl.ds(aligned(cc, cb), cb)
        right = col_s[here, :]
        right_sq = jnp.sum(jnp.where(diag, squares(right), 0.0), axis=0, keepdims=True)
        vec = col_vec[here, :]

        def row_chunk(rc):
            there = pl.ds(aligned(rc, rb), rb)
            kern = kerns(row_s[there, :], right, right_sq)
            prod = jnp.dot(kern, vec, preferred_element_type=F32)
            mine = row_vec[there, :]
            forms = [jnp.sum(mine * prod[b * rb:(b + 1) * rb], axis=0, keepdims=True) for b in range(n_bands)]
            add_to(pl.ds(0, n_vec), jnp.concatenate(forms, axis=0))
            kern = kerns(row_c[there, :], right, right_sq)
            flat = lax.dot_general(vec[:, :128], kern, (((0,), (1,)), ((), ())), preferred_element_type=F32)
            proof = jnp.concatenate([flat[0:1, b * rb:(b + 1) * rb] for b in range(n_bands)], axis=0)
            add_to(pl.ds(aligned(rc, rb) + n_vec, rb), proof)

        loop(rows // rb, row_chunk)

    loop(cols // cb, column_chunk)

    pl.semaphore_wait(pair_sem, 1)
    for t in range(1, n_plane):
        to = (pslot + t) % n_plane
        c = remote(part1.at[pslot], part1.at[pslot], p1_send.at[t], p1_recv.at[pslot],
                   at_row(to // CORES, to % CORES))
        c.start()
        sends.append(c)
    for t in range(1, n_plane):
        src = (pslot + n_plane - t) % n_plane
        remote(part1.at[src], part1.at[src], p1_send.at[t], p1_recv.at[src],
               at_row(src // CORES, src % CORES)).wait_recv()
    quad = part1[0, :, :n_vec]
    for slot in range(1, n_plane):
        quad = quad + part1[slot, :, :n_vec]
    part2[z] = quad
    for t in range(1, n_hi):
        to = (z + t) % n_hi
        c = remote(part2.at[z], part2.at[z], p2_send.at[t], p2_recv.at[z], at_col(to, core))
        c.start()
        sends.append(c)
    proof = part1[core, :, n_vec:]
    for slot in range(1, n_row):
        proof = proof + part1[slot * CORES + core, :, n_vec:]
    mine = jnp.zeros((n_bands, own), F32)
    for slot in range(n_row):
        mine = jnp.where(rslot == slot, proof[:, slot * own:(slot + 1) * own], mine)
    proof_out[...] = mine * F32(1.0 / math.sqrt(total))
    for t in range(1, n_hi):
        src = (z + n_hi - t) % n_hi
        remote(part2.at[src], part2.at[src], p2_send.at[t], p2_recv.at[src], at_col(src, core)).wait_recv()
    quad = part2[0]
    for slot in range(1, n_hi):
        quad = quad + part2[slot]
    quad = quad * F32(1.0 / total)
    quad_out[...] = quad
    boot = lax.broadcasted_iota(jnp.int32, quad.shape, 1) > 0
    count = F32(1.0 / (n_vec - 1))
    centre = jnp.sum(jnp.where(boot, quad, 0.0), axis=1, keepdims=True) * count
    off = quad - centre
    spread = jnp.sum(jnp.where(boot, off * off, 0.0), axis=1, keepdims=True) * count
    score = (quad[:, :1] - centre) / jnp.sqrt(spread + 1e-6)
    spot = lax.broadcasted_iota(jnp.int32, (n_bands, n_bands), 0) == lax.broadcasted_iota(
        jnp.int32, (n_bands, n_bands), 1)
    score_out[...] = jnp.sum(jnp.where(spot, score, 0.0), axis=0, keepdims=True)
    for c in sends:
        c.wait_send()
    for cond, c in cond_sends:
        pl.when(cond)(c.wait_send)


def per_device(n_grp, n_dev, samples, labels, words, corpus, grid, pick):
    n_lo = 2 if n_dev % 2 == 0 else 1
    n_gx, n_hi = n_grp // CORES, n_dev // n_lo
    n_row, n_col, n_plane = n_gx * n_lo, n_hi * CORES, n_gx * n_lo * CORES
    own, width = samples.shape
    rows, cols = n_row * own, n_col * own
    n_bands, n_vec = pick.shape[0], 512
    dma = lambda *n: pltpu.SemaphoreType.DMA(n)
    any_ = pl.BlockSpec(memory_space=pl.ANY)
    vmem = pl.BlockSpec(memory_space=pltpu.VMEM)
    quad, score, proof = pl.pallas_call(
        functools.partial(kernel, (n_gx, n_lo, n_hi)),
        out_shape=(
            jax.ShapeDtypeStruct((n_bands, n_vec), F32),
            jax.ShapeDtypeStruct((1, n_bands), F32),
            jax.ShapeDtypeStruct((n_bands, own), F32),
        ),
        in_specs=[any_] * 6,
        out_specs=(vmem, vmem, vmem),
        scratch_shapes=[
            pltpu.VMEM((rows, width), BF16),
            pltpu.VMEM((rows, width), BF16),
            pltpu.VMEM((cols, width), BF16),
            pltpu.VMEM(words.shape, jnp.int32),
            pltpu.VMEM((1, own), jnp.int32),
            pltpu.SMEM(grid.shape, F32),
            pltpu.SMEM(pick.shape, jnp.int32),
            pltpu.VMEM((n_row, 8, 128), jnp.int32),
            pltpu.VMEM((n_col, 8, 128), jnp.int32),
            pltpu.VMEM((rows, n_vec), F32),
            pltpu.VMEM((cols, n_vec), BF16),
            pltpu.VMEM((n_plane, n_bands, n_vec + rows), F32),
            pltpu.VMEM((n_hi, n_bands, n_vec), F32),
            pltpu.SemaphoreType.REGULAR,
            dma(7),
            dma(n_row, n_row), dma(n_row), dma(n_row, n_row), dma(n_row), dma(n_row, n_row), dma(n_row),
            dma(2, n_hi), dma(n_hi), dma(2, n_hi), dma(n_hi), dma(n_hi), dma(n_hi), dma(n_hi), dma(n_hi),
            dma(n_plane), dma(n_plane), dma(n_hi), dma(n_hi),
        ],
        compiler_params=pltpu.CompilerParams(
            collective_id=0, has_side_effects=True, vmem_limit_bytes=62 * 1024 * 1024),
        name="two_sample",
    )(samples, labels.reshape(1, own), words, corpus, grid, pick)
    return quad, score.reshape(n_bands), proof


def solution(mesh):
    in_specs = (
        P(("grp", "dev"), None),
        P(("grp", "dev")),
        P(("grp", "dev"), None),
        P(("grp", "dev"), None),
        P(),
        P(),
    )
    out_specs = (P(), P(), P(None, ("grp", "dev")))
    return jax.shard_map(
        functools.partial(per_device, mesh.shape["grp"], mesh.shape["dev"]),
        mesh=mesh, in_specs=in_specs, out_specs=out_specs, check_vma=False
    )
```

```python
import functools
import math

import jax
import jax.numpy as jnp
from jax import lax
from jax.experimental import pallas as pl
from jax.experimental.pallas import tpu as pltpu
from jax.sharding import PartitionSpec as P

WORD_BITS = 21
CORES = 2
LOG2E = math.log2(math.e)
MESH = pl.DeviceIdType.MESH
F32 = jnp.float32
BF16 = jnp.bfloat16


def loop(count, body):
    if count == 1:
        body(0)
    else:
        lax.fori_loop(0, count, lambda i, c: (body(i), c)[1], 0)


def aligned(index, size):
    return index * size if isinstance(index, int) else pl.multiple_of(index * size, size)


def kernel(geo, samples, labels, words, corpus, grid, pick, quad_out, score_out, proof_out,
           row_s, row_c, col_s, word_in, label_in, grid_in, pick_in, row_pack, col_pack, row_vec, col_vec,
           part1, part2, local_sem, rp_send, rp_recv, cp_send, cp_recv, rs_send, rs_recv,
           rc_send, rc_recv, cs_send, cs_recv, fw_send, fw_recv, p1_send, p1_recv, p2_send, p2_recv):
    n_gx, n_lo, n_hi = geo
    own = samples.shape[0]
    n_bands, n_vec = quad_out.shape
    n_row, n_col, n_plane = n_gx * n_lo, n_hi * CORES, n_gx * n_lo * CORES
    rows, cols = n_row * own, n_col * own
    n_words = words.shape[1]
    total = n_row * n_col * own

    grp, dev = lax.axis_index("grp"), lax.axis_index("dev")
    gx, core = grp // CORES, grp % CORES
    z, lo = dev // n_lo, dev % n_lo
    other = 1 - core
    rslot = gx * n_lo + lo
    cslot = z * CORES + core
    pslot = rslot * CORES + core

    def at_row(slot, core_):
        return ((slot // n_lo) * CORES + core_, z * n_lo + slot % n_lo)

    def at_col(z_, core_):
        return (gx * CORES + core_, z_ * n_lo + lo)

    barrier = pltpu.get_barrier_semaphore()
    partners = []
    for t in range(1, n_plane):
        slot = (pslot + t) % n_plane
        partners.append(at_row(slot // CORES, slot % CORES))
    for t in range(1, n_hi):
        partners.append(at_col((z + t) % n_hi, core))
        partners.append(at_col((z + t) % n_hi, other))

    word_copy = pltpu.make_async_copy(words, word_in, local_sem.at[0])
    label_copy = pltpu.make_async_copy(labels, label_in, local_sem.at[1])
    word_copy.start()
    label_copy.start()
    for p in partners:
        pl.semaphore_signal(barrier, inc=1, device_id=p, device_id_type=MESH)
    own_rows = pl.ds(pl.multiple_of(rslot * own, own), own)
    own_cols = pl.ds(pl.multiple_of(cslot * own, own), own)
    keep = [
        pltpu.make_async_copy(samples, row_s.at[own_rows], local_sem.at[2]),
        pltpu.make_async_copy(corpus, row_c.at[own_rows], local_sem.at[3]),
        pltpu.make_async_copy(samples, col_s.at[own_cols], local_sem.at[4]),
        pltpu.make_async_copy(grid, grid_in, local_sem.at[5]),
        pltpu.make_async_copy(pick, pick_in, local_sem.at[6]),
    ]
    for c in keep:
        c.start()


    word_copy.wait()
    label_copy.wait()
    eye = lax.broadcasted_iota(jnp.int32, (own, own), 0) == lax.broadcasted_iota(jnp.int32, (own, own), 1)
    label_col = jnp.sum(jnp.where(eye, label_in[...].astype(F32), 0.0), axis=1, keepdims=True).astype(jnp.int32)
    groups = own // 8
    pieces = []
    width = 128 // groups
    for q in range(groups):
        pieces.append(word_in[pl.ds(8 * q, 8), :])
        pieces.append(label_col[8 * q:8 * q + 8])
        pieces.append(jnp.zeros((8, width - n_words - 1), jnp.int32))
    packed = jnp.concatenate(pieces, axis=1)
    col_pack[cslot] = packed
    row_pack[rslot] = packed

    pl.semaphore_wait(barrier, len(partners))

    def remote(src, dst, send, recv, to):
        return pltpu.make_async_remote_copy(
            src_ref=src, dst_ref=dst, send_sem=send, recv_sem=recv, device_id=to, device_id_type=MESH)

    sends = []
    col_in, fw_in, rs_in, rc_in = [], [], [], []

    def col_block(slot):
        return col_s.at[pl.ds(pl.multiple_of(slot * own, own), own)]

    def row_block(ref, slot):
        return ref.at[pl.ds(pl.multiple_of(slot * own, own), own)]

    for t in range(1, n_col):
        to = (cslot + t) % n_col
        c = remote(col_pack.at[cslot], col_pack.at[cslot], cp_send.at[t], cp_recv.at[cslot],
                   at_col(to // CORES, to % CORES))
        c.start()
        sends.append(c)
    for t in range(1, n_row):
        to = (rslot + t) % n_row
        c = remote(row_pack.at[rslot], row_pack.at[rslot], rp_send.at[t], rp_recv.at[rslot], at_row(to, core))
        c.start()
        sends.append(c)
    for t in range(1, n_hi):
        to = (z + t) % n_hi
        c = remote(samples, col_block(cslot), cs_send.at[t], cs_recv.at[z], at_col(to, core))
        c.start()
        sends.append(c)
    for t in range(1, n_row):
        to = (rslot + t) % n_row
        c = remote(samples, row_block(row_s, rslot), rs_send.at[t], rs_recv.at[rslot], at_row(to, core))
        c.start()
        sends.append(c)
    c = remote(samples, col_block(cslot), fw_send.at[z], fw_recv.at[z], at_col(z, other))
    c.start()
    sends.append(c)

    for t in range(1, n_row):
        to = (rslot + t) % n_row
        c = remote(corpus, row_block(row_c, rslot), rc_send.at[t], rc_recv.at[rslot], at_row(to, core))
        c.start()
        sends.append(c)

    for t in range(1, n_hi):
        src = (z + n_hi - t) % n_hi
        block = col_block(src * CORES + core)
        remote(samples, block, cs_send.at[t], cs_recv.at[src], at_col(src, core)).wait_recv()
        c = remote(block, block, fw_send.at[src], fw_recv.at[src], at_col(z, other))
        c.start()
        sends.append(c)

    lane = lax.broadcasted_iota(jnp.int32, (8, 128), 1)
    label_lane = lane - lane % width + n_words
    is_label = lane % width == n_words
    n_chunks = n_vec // 128
    index, mask = [], []
    for t in range(n_chunks):
        k = jnp.maximum(lane + (128 * t - 1), 0)
        w = (k * 3121) >> 16
        shift = k - w * WORD_BITS
        if t == 0:
            w = jnp.where(lane == 0, n_words, w)
            shift = jnp.where(lane == 0, 0, shift)
        index.append(w)
        mask.append(jnp.int32(1) << shift)

    def expand(tile, dst, base):
        label = jnp.take_along_axis(tile, label_lane, axis=1)
        tile = jnp.where(is_label, label ^ 1, tile ^ (0 - label))
        for t in range(n_chunks):
            parts = []
            for q in range(groups):
                got = jnp.take_along_axis(tile, index[t] + q * width, axis=1)
                parts.append(jnp.where((got & mask[t]) != 0, 1.0, -1.0).astype(F32))
            dst[pl.ds(base, own), pl.ds(128 * t, 128)] = jnp.concatenate(parts, axis=0).astype(dst.dtype)

    for t in range(1, n_col):
        src = (cslot + n_col - t) % n_col
        remote(col_pack.at[src], col_pack.at[src], cp_send.at[t], cp_recv.at[src],
               at_col(src // CORES, src % CORES)).wait_recv()
    for t in range(1, n_row):
        src = (rslot + n_row - t) % n_row
        remote(row_pack.at[src], row_pack.at[src], rp_send.at[t], rp_recv.at[src], at_row(src, core)).wait_recv()
    for slot in range(n_col):
        expand(col_pack[slot], col_vec, slot * own)
    for slot in range(n_row):
        expand(row_pack[slot], row_vec, slot * own)

    for c in keep:
        c.wait()
    for t in range(n_hi):
        src = (z + n_hi - t) % n_hi
        block = col_block(src * CORES + other)
        remote(samples, block, fw_send.at[src], fw_recv.at[src], at_col(z, other)).wait_recv()
    for t in range(1, n_row):
        src = (rslot + n_row - t) % n_row
        remote(samples, row_block(row_s, src), rs_send.at[t], rs_recv.at[src], at_row(src, core)).wait_recv()
    for t in range(1, n_row):
        src = (rslot + n_row - t) % n_row
        remote(corpus, row_block(row_c, src), rc_send.at[t], rc_recv.at[src], at_row(src, core)).wait_recv()

    rb, cb = min(128, rows), min(256, cols)
    gains = [jnp.full((1, 1), -0.5 * LOG2E, F32) / jnp.full((1, 1), grid_in[pick_in[b]], F32) for b in range(n_bands)]
    diag = lax.broadcasted_iota(jnp.int32, (cb, cb), 0) == lax.broadcasted_iota(jnp.int32, (cb, cb), 1)
    if rows > rb or cols > cb:
        part1[pslot] = jnp.zeros(part1.shape[1:], F32)

    def squares(x):
        wide = x.astype(F32)
        return jnp.sum(wide * wide, axis=1, keepdims=True)

    def kerns(left, right, right_sq):
        cross = lax.dot_general(left, right, (((1,), (1,)), ((), ())), preferred_element_type=F32)
        dist = squares(left) + right_sq - 2.0 * cross
        return jnp.concatenate([jnp.exp2(dist * g).astype(BF16) for g in gains], axis=0)

    def add_to(lanes, value):
        if rows > rb or cols > cb:
            value = part1[pslot, :, lanes] + value
        part1[pslot, :, lanes] = value

    def column_chunk(cc):
        here = pl.ds(aligned(cc, cb), cb)
        right = col_s[here, :]
        right_sq = jnp.sum(jnp.where(diag, squares(right), 0.0), axis=0, keepdims=True)
        vec = col_vec[here, :]

        def row_chunk(rc):
            there = pl.ds(aligned(rc, rb), rb)
            kern = kerns(row_s[there, :], right, right_sq)
            prod = jnp.dot(kern, vec, preferred_element_type=F32)
            mine = row_vec[there, :]
            forms = [jnp.sum(mine * prod[b * rb:(b + 1) * rb], axis=0, keepdims=True) for b in range(n_bands)]
            add_to(pl.ds(0, n_vec), jnp.concatenate(forms, axis=0))
            kern = kerns(row_c[there, :], right, right_sq)
            flat = lax.dot_general(vec[:, :128], kern, (((0,), (1,)), ((), ())), preferred_element_type=F32)
            proof = jnp.concatenate([flat[0:1, b * rb:(b + 1) * rb] for b in range(n_bands)], axis=0)
            add_to(pl.ds(aligned(rc, rb) + n_vec, rb), proof)

        loop(rows // rb, row_chunk)

    loop(cols // cb, column_chunk)

    for t in range(1, n_plane):
        to = (pslot + t) % n_plane
        c = remote(part1.at[pslot], part1.at[pslot], p1_send.at[t], p1_recv.at[pslot],
                   at_row(to // CORES, to % CORES))
        c.start()
        sends.append(c)
    for t in range(1, n_plane):
        src = (pslot + n_plane - t) % n_plane
        remote(part1.at[src], part1.at[src], p1_send.at[t], p1_recv.at[src],
               at_row(src // CORES, src % CORES)).wait_recv()
    quad = part1[0, :, :n_vec]
    for slot in range(1, n_plane):
        quad = quad + part1[slot, :, :n_vec]
    part2[z] = quad
    for t in range(1, n_hi):
        to = (z + t) % n_hi
        c = remote(part2.at[z], part2.at[z], p2_send.at[t], p2_recv.at[z], at_col(to, core))
        c.start()
        sends.append(c)
    proof = part1[core, :, n_vec:]
    for slot in range(1, n_row):
        proof = proof + part1[slot * CORES + core, :, n_vec:]
    mine = jnp.zeros((n_bands, own), F32)
    for slot in range(n_row):
        mine = jnp.where(rslot == slot, proof[:, slot * own:(slot + 1) * own], mine)
    proof_out[...] = mine * F32(1.0 / math.sqrt(total))
    for t in range(1, n_hi):
        src = (z + n_hi - t) % n_hi
        remote(part2.at[src], part2.at[src], p2_send.at[t], p2_recv.at[src], at_col(src, core)).wait_recv()
    quad = part2[0]
    for slot in range(1, n_hi):
        quad = quad + part2[slot]
    quad = quad * F32(1.0 / total)
    quad_out[...] = quad
    boot = lax.broadcasted_iota(jnp.int32, quad.shape, 1) > 0
    count = F32(1.0 / (n_vec - 1))
    centre = jnp.sum(jnp.where(boot, quad, 0.0), axis=1, keepdims=True) * count
    off = quad - centre
    spread = jnp.sum(jnp.where(boot, off * off, 0.0), axis=1, keepdims=True) * count
    score = (quad[:, :1] - centre) / jnp.sqrt(spread + 1e-6)
    spot = lax.broadcasted_iota(jnp.int32, (n_bands, n_bands), 0) == lax.broadcasted_iota(
        jnp.int32, (n_bands, n_bands), 1)
    score_out[...] = jnp.sum(jnp.where(spot, score, 0.0), axis=0, keepdims=True)
    for c in sends:
        c.wait_send()


def per_device(n_grp, n_dev, samples, labels, words, corpus, grid, pick):
    n_lo = 2 if n_dev % 2 == 0 else 1
    n_gx, n_hi = n_grp // CORES, n_dev // n_lo
    n_row, n_col, n_plane = n_gx * n_lo, n_hi * CORES, n_gx * n_lo * CORES
    own, width = samples.shape
    rows, cols = n_row * own, n_col * own
    n_bands, n_vec = pick.shape[0], 512
    dma = lambda n: pltpu.SemaphoreType.DMA((n,))
    any_ = pl.BlockSpec(memory_space=pl.ANY)
    vmem = pl.BlockSpec(memory_space=pltpu.VMEM)
    quad, score, proof = pl.pallas_call(
        functools.partial(kernel, (n_gx, n_lo, n_hi)),
        out_shape=(
            jax.ShapeDtypeStruct((n_bands, n_vec), F32),
            jax.ShapeDtypeStruct((1, n_bands), F32),
            jax.ShapeDtypeStruct((n_bands, own), F32),
        ),
        in_specs=[any_] * 6,
        out_specs=(vmem, vmem, vmem),
        scratch_shapes=[
            pltpu.VMEM((rows, width), BF16),
            pltpu.VMEM((rows, width), BF16),
            pltpu.VMEM((cols, width), BF16),
            pltpu.VMEM(words.shape, jnp.int32),
            pltpu.VMEM((1, own), jnp.int32),
            pltpu.SMEM(grid.shape, F32),
            pltpu.SMEM(pick.shape, jnp.int32),
            pltpu.VMEM((n_row, 8, 128), jnp.int32),
            pltpu.VMEM((n_col, 8, 128), jnp.int32),
            pltpu.VMEM((rows, n_vec), F32),
            pltpu.VMEM((cols, n_vec), BF16),
            pltpu.VMEM((n_plane, n_bands, n_vec + rows), F32),
            pltpu.VMEM((n_hi, n_bands, n_vec), F32),
            dma(7),
            dma(n_row), dma(n_row), dma(n_col), dma(n_col), dma(n_row), dma(n_row),
            dma(n_row), dma(n_row), dma(n_hi), dma(n_hi), dma(n_hi), dma(n_hi),
            dma(n_plane), dma(n_plane), dma(n_hi), dma(n_hi),
        ],
        compiler_params=pltpu.CompilerParams(
            collective_id=0, has_side_effects=True, vmem_limit_bytes=62 * 1024 * 1024),
        name="two_sample",
    )(samples, labels.reshape(1, own), words, corpus, grid, pick)
    return quad, score.reshape(n_bands), proof


def solution(mesh):
    in_specs = (
        P(("grp", "dev"), None),
        P(("grp", "dev")),
        P(("grp", "dev"), None),
        P(("grp", "dev"), None),
        P(),
        P(),
    )
    out_specs = (P(), P(), P(None, ("grp", "dev")))
    return jax.shard_map(
        functools.partial(per_device, mesh.shape["grp"], mesh.shape["dev"]),
        mesh=mesh, in_specs=in_specs, out_specs=out_specs, check_vma=False
    )
```

```python
import functools
import math

import jax
import jax.numpy as jnp
from jax import lax
from jax.experimental import pallas as pl
from jax.experimental.pallas import tpu as pltpu
from jax.sharding import PartitionSpec as P

WORD_BITS = 21
CORES = 2
LOG2E = math.log2(math.e)
MESH = pl.DeviceIdType.MESH
F32 = jnp.float32
BF16 = jnp.bfloat16


def loop(count, body):
    if count == 1:
        body(0)
    else:
        lax.fori_loop(0, count, lambda i, c: (body(i), c)[1], 0)


def aligned(index, size):
    return index * size if isinstance(index, int) else pl.multiple_of(index * size, size)


def kernel(geo, samples, labels, words, corpus, grid, pick, quad_out, proof_out,
           row_s, row_c, col_s, word_in, label_in, grid_in, pick_in, row_pack, col_pack, row_vec, col_vec,
           part1, part2, local_sem, rp_send, rp_recv, cp_send, cp_recv, rs_send, rs_recv,
           rc_send, rc_recv, cs_send, cs_recv, fw_send, fw_recv, p1_send, p1_recv, p2_send, p2_recv):
    n_gx, n_lo, n_hi = geo
    own = samples.shape[0]
    n_bands, n_vec = quad_out.shape
    n_row, n_col, n_plane = n_gx * n_lo, n_hi * CORES, n_gx * n_lo * CORES
    rows, cols = n_row * own, n_col * own
    n_words = words.shape[1]
    total = n_row * n_col * own

    grp, dev = lax.axis_index("grp"), lax.axis_index("dev")
    gx, core = grp // CORES, grp % CORES
    z, lo = dev // n_lo, dev % n_lo
    other = 1 - core
    rslot = gx * n_lo + lo
    cslot = z * CORES + core
    pslot = rslot * CORES + core

    def at_row(slot, core_):
        return ((slot // n_lo) * CORES + core_, z * n_lo + slot % n_lo)

    def at_col(z_, core_):
        return (gx * CORES + core_, z_ * n_lo + lo)

    barrier = pltpu.get_barrier_semaphore()
    partners = []
    for t in range(1, n_plane):
        slot = (pslot + t) % n_plane
        partners.append(at_row(slot // CORES, slot % CORES))
    for t in range(1, n_hi):
        partners.append(at_col((z + t) % n_hi, core))
        partners.append(at_col((z + t) % n_hi, other))

    word_copy = pltpu.make_async_copy(words, word_in, local_sem.at[0])
    label_copy = pltpu.make_async_copy(labels, label_in, local_sem.at[1])
    word_copy.start()
    label_copy.start()
    for p in partners:
        pl.semaphore_signal(barrier, inc=1, device_id=p, device_id_type=MESH)
    own_rows = pl.ds(pl.multiple_of(rslot * own, own), own)
    own_cols = pl.ds(pl.multiple_of(cslot * own, own), own)
    keep = [
        pltpu.make_async_copy(samples, row_s.at[own_rows], local_sem.at[2]),
        pltpu.make_async_copy(corpus, row_c.at[own_rows], local_sem.at[3]),
        pltpu.make_async_copy(samples, col_s.at[own_cols], local_sem.at[4]),
        pltpu.make_async_copy(grid, grid_in, local_sem.at[5]),
        pltpu.make_async_copy(pick, pick_in, local_sem.at[6]),
    ]
    for c in keep:
        c.start()


    word_copy.wait()
    label_copy.wait()
    eye = lax.broadcasted_iota(jnp.int32, (own, own), 0) == lax.broadcasted_iota(jnp.int32, (own, own), 1)
    label_col = jnp.sum(jnp.where(eye, label_in[...].astype(F32), 0.0), axis=1, keepdims=True).astype(jnp.int32)
    groups = own // 8
    pieces = []
    width = 128 // groups
    for q in range(groups):
        pieces.append(word_in[pl.ds(8 * q, 8), :])
        pieces.append(label_col[8 * q:8 * q + 8])
        pieces.append(jnp.zeros((8, width - n_words - 1), jnp.int32))
    packed = jnp.concatenate(pieces, axis=1)
    col_pack[cslot] = packed
    row_pack[rslot] = packed

    pl.semaphore_wait(barrier, len(partners))

    def remote(src, dst, send, recv, to):
        return pltpu.make_async_remote_copy(
            src_ref=src, dst_ref=dst, send_sem=send, recv_sem=recv, device_id=to, device_id_type=MESH)

    sends = []
    col_in, fw_in, rs_in, rc_in = [], [], [], []

    def col_block(slot):
        return col_s.at[pl.ds(pl.multiple_of(slot * own, own), own)]

    def row_block(ref, slot):
        return ref.at[pl.ds(pl.multiple_of(slot * own, own), own)]

    for t in range(1, n_col):
        to = (cslot + t) % n_col
        c = remote(col_pack.at[cslot], col_pack.at[cslot], cp_send.at[t], cp_recv.at[cslot],
                   at_col(to // CORES, to % CORES))
        c.start()
        sends.append(c)
    for t in range(1, n_row):
        to = (rslot + t) % n_row
        c = remote(row_pack.at[rslot], row_pack.at[rslot], rp_send.at[t], rp_recv.at[rslot], at_row(to, core))
        c.start()
        sends.append(c)
    for t in range(1, n_hi):
        to = (z + t) % n_hi
        c = remote(samples, col_block(cslot), cs_send.at[t], cs_recv.at[z], at_col(to, core))
        c.start()
        sends.append(c)
    for t in range(1, n_row):
        to = (rslot + t) % n_row
        c = remote(samples, row_block(row_s, rslot), rs_send.at[t], rs_recv.at[rslot], at_row(to, core))
        c.start()
        sends.append(c)
    c = remote(samples, col_block(cslot), fw_send.at[z], fw_recv.at[z], at_col(z, other))
    c.start()
    sends.append(c)

    for t in range(1, n_row):
        to = (rslot + t) % n_row
        c = remote(corpus, row_block(row_c, rslot), rc_send.at[t], rc_recv.at[rslot], at_row(to, core))
        c.start()
        sends.append(c)

    for t in range(1, n_hi):
        src = (z + n_hi - t) % n_hi
        block = col_block(src * CORES + core)
        remote(samples, block, cs_send.at[t], cs_recv.at[src], at_col(src, core)).wait_recv()
        c = remote(block, block, fw_send.at[src], fw_recv.at[src], at_col(z, other))
        c.start()
        sends.append(c)

    lane = lax.broadcasted_iota(jnp.int32, (8, 128), 1)
    label_lane = lane - lane % width + n_words
    is_label = lane % width == n_words
    n_chunks = n_vec // 128
    index, mask = [], []
    for t in range(n_chunks):
        k = jnp.maximum(lane + (128 * t - 1), 0)
        w = (k * 3121) >> 16
        shift = k - w * WORD_BITS
        if t == 0:
            w = jnp.where(lane == 0, n_words, w)
            shift = jnp.where(lane == 0, 0, shift)
        index.append(w)
        mask.append(jnp.int32(1) << shift)

    def expand(tile, dst, base):
        label = jnp.take_along_axis(tile, label_lane, axis=1)
        tile = jnp.where(is_label, label ^ 1, tile ^ (0 - label))
        for t in range(n_chunks):
            parts = []
            for q in range(groups):
                got = jnp.take_along_axis(tile, index[t] + q * width, axis=1)
                parts.append(jnp.where((got & mask[t]) != 0, 1.0, -1.0).astype(F32))
            dst[pl.ds(base, own), pl.ds(128 * t, 128)] = jnp.concatenate(parts, axis=0).astype(dst.dtype)

    for t in range(1, n_col):
        src = (cslot + n_col - t) % n_col
        remote(col_pack.at[src], col_pack.at[src], cp_send.at[t], cp_recv.at[src],
               at_col(src // CORES, src % CORES)).wait_recv()
    for t in range(1, n_row):
        src = (rslot + n_row - t) % n_row
        remote(row_pack.at[src], row_pack.at[src], rp_send.at[t], rp_recv.at[src], at_row(src, core)).wait_recv()
    for slot in range(n_col):
        expand(col_pack[slot], col_vec, slot * own)
    for slot in range(n_row):
        expand(row_pack[slot], row_vec, slot * own)

    for c in keep:
        c.wait()
    for t in range(n_hi):
        src = (z + n_hi - t) % n_hi
        block = col_block(src * CORES + other)
        remote(samples, block, fw_send.at[src], fw_recv.at[src], at_col(z, other)).wait_recv()
    for t in range(1, n_row):
        src = (rslot + n_row - t) % n_row
        remote(samples, row_block(row_s, src), rs_send.at[t], rs_recv.at[src], at_row(src, core)).wait_recv()
    for t in range(1, n_row):
        src = (rslot + n_row - t) % n_row
        remote(corpus, row_block(row_c, src), rc_send.at[t], rc_recv.at[src], at_row(src, core)).wait_recv()

    rb, cb = min(128, rows), min(256, cols)
    gains = [jnp.full((1, 1), -0.5 * LOG2E, F32) / jnp.full((1, 1), grid_in[pick_in[b]], F32) for b in range(n_bands)]
    diag = lax.broadcasted_iota(jnp.int32, (cb, cb), 0) == lax.broadcasted_iota(jnp.int32, (cb, cb), 1)
    if rows > rb or cols > cb:
        part1[pslot] = jnp.zeros(part1.shape[1:], F32)

    def squares(x):
        wide = x.astype(F32)
        return jnp.sum(wide * wide, axis=1, keepdims=True)

    def kerns(left, right, right_sq):
        cross = lax.dot_general(left, right, (((1,), (1,)), ((), ())), preferred_element_type=F32)
        dist = squares(left) + right_sq - 2.0 * cross
        return jnp.concatenate([jnp.exp2(dist * g).astype(BF16) for g in gains], axis=0)

    def add_to(lanes, value):
        if rows > rb or cols > cb:
            value = part1[pslot, :, lanes] + value
        part1[pslot, :, lanes] = value

    def column_chunk(cc):
        here = pl.ds(aligned(cc, cb), cb)
        right = col_s[here, :]
        right_sq = jnp.sum(jnp.where(diag, squares(right), 0.0), axis=0, keepdims=True)
        vec = col_vec[here, :]

        def row_chunk(rc):
            there = pl.ds(aligned(rc, rb), rb)
            kern = kerns(row_s[there, :], right, right_sq)
            prod = jnp.dot(kern, vec, preferred_element_type=F32)
            mine = row_vec[there, :]
            forms = [jnp.sum(mine * prod[b * rb:(b + 1) * rb], axis=0, keepdims=True) for b in range(n_bands)]
            add_to(pl.ds(0, n_vec), jnp.concatenate(forms, axis=0))
            kern = kerns(row_c[there, :], right, right_sq)
            flat = lax.dot_general(vec[:, :128], kern, (((0,), (1,)), ((), ())), preferred_element_type=F32)
            proof = jnp.concatenate([flat[0:1, b * rb:(b + 1) * rb] for b in range(n_bands)], axis=0)
            add_to(pl.ds(aligned(rc, rb) + n_vec, rb), proof)

        loop(rows // rb, row_chunk)

    loop(cols // cb, column_chunk)

    for t in range(1, n_plane):
        to = (pslot + t) % n_plane
        c = remote(part1.at[pslot], part1.at[pslot], p1_send.at[t], p1_recv.at[pslot],
                   at_row(to // CORES, to % CORES))
        c.start()
        sends.append(c)
    for t in range(1, n_plane):
        src = (pslot + n_plane - t) % n_plane
        remote(part1.at[src], part1.at[src], p1_send.at[t], p1_recv.at[src],
               at_row(src // CORES, src % CORES)).wait_recv()
    quad = part1[0, :, :n_vec]
    for slot in range(1, n_plane):
        quad = quad + part1[slot, :, :n_vec]
    part2[z] = quad
    for t in range(1, n_hi):
        to = (z + t) % n_hi
        c = remote(part2.at[z], part2.at[z], p2_send.at[t], p2_recv.at[z], at_col(to, core))
        c.start()
        sends.append(c)
    proof = part1[core, :, n_vec:]
    for slot in range(1, n_row):
        proof = proof + part1[slot * CORES + core, :, n_vec:]
    mine = jnp.zeros((n_bands, own), F32)
    for slot in range(n_row):
        mine = jnp.where(rslot == slot, proof[:, slot * own:(slot + 1) * own], mine)
    proof_out[...] = mine * F32(1.0 / math.sqrt(total))
    for t in range(1, n_hi):
        src = (z + n_hi - t) % n_hi
        remote(part2.at[src], part2.at[src], p2_send.at[t], p2_recv.at[src], at_col(src, core)).wait_recv()
    quad = part2[0]
    for slot in range(1, n_hi):
        quad = quad + part2[slot]
    quad = quad * F32(1.0 / total)
    quad_out[...] = quad
    for c in sends:
        c.wait_send()


def finish(quad_in, proof_in, quad_out, score_out, proof_out):
    quad = quad_in[...]
    quad_out[...] = quad
    proof_out[...] = proof_in[...]
    n_bands, n_vec = quad.shape
    boot = lax.broadcasted_iota(jnp.int32, quad.shape, 1) > 0
    count = F32(1.0 / (n_vec - 1))
    centre = jnp.sum(jnp.where(boot, quad, 0.0), axis=1, keepdims=True) * count
    off = quad - centre
    spread = jnp.sum(jnp.where(boot, off * off, 0.0), axis=1, keepdims=True) * count
    score = (quad[:, :1] - centre) / jnp.sqrt(spread + 1e-6)
    spot = lax.broadcasted_iota(jnp.int32, (n_bands, n_bands), 0) == lax.broadcasted_iota(
        jnp.int32, (n_bands, n_bands), 1)
    score_out[...] = jnp.sum(jnp.where(spot, score, 0.0), axis=0, keepdims=True)


def per_device(n_grp, n_dev, samples, labels, words, corpus, grid, pick):
    n_lo = 2 if n_dev % 2 == 0 else 1
    n_gx, n_hi = n_grp // CORES, n_dev // n_lo
    n_row, n_col, n_plane = n_gx * n_lo, n_hi * CORES, n_gx * n_lo * CORES
    own, width = samples.shape
    rows, cols = n_row * own, n_col * own
    n_bands, n_vec = pick.shape[0], 512
    dma = lambda n: pltpu.SemaphoreType.DMA((n,))
    any_ = pl.BlockSpec(memory_space=pl.ANY)
    vmem = pl.BlockSpec(memory_space=pltpu.VMEM)
    quad, proof = pl.pallas_call(
        functools.partial(kernel, (n_gx, n_lo, n_hi)),
        out_shape=(
            jax.ShapeDtypeStruct((n_bands, n_vec), F32),
            jax.ShapeDtypeStruct((n_bands, own), F32),
        ),
        in_specs=[any_] * 6,
        out_specs=(vmem, vmem),
        scratch_shapes=[
            pltpu.VMEM((rows, width), BF16),
            pltpu.VMEM((rows, width), BF16),
            pltpu.VMEM((cols, width), BF16),
            pltpu.VMEM(words.shape, jnp.int32),
            pltpu.VMEM((1, own), jnp.int32),
            pltpu.SMEM(grid.shape, F32),
            pltpu.SMEM(pick.shape, jnp.int32),
            pltpu.VMEM((n_row, 8, 128), jnp.int32),
            pltpu.VMEM((n_col, 8, 128), jnp.int32),
            pltpu.VMEM((rows, n_vec), F32),
            pltpu.VMEM((cols, n_vec), BF16),
            pltpu.VMEM((n_plane, n_bands, n_vec + rows), F32),
            pltpu.VMEM((n_hi, n_bands, n_vec), F32),
            dma(7),
            dma(n_row), dma(n_row), dma(n_col), dma(n_col), dma(n_row), dma(n_row),
            dma(n_row), dma(n_row), dma(n_hi), dma(n_hi), dma(n_hi), dma(n_hi),
            dma(n_plane), dma(n_plane), dma(n_hi), dma(n_hi),
        ],
        compiler_params=pltpu.CompilerParams(
            collective_id=0, has_side_effects=True, vmem_limit_bytes=62 * 1024 * 1024),
        name="two_sample",
    )(samples, labels.reshape(1, own), words, corpus, grid, pick)
    quad, score, proof = pl.pallas_call(
        finish,
        out_shape=(
            jax.ShapeDtypeStruct((n_bands, n_vec), F32),
            jax.ShapeDtypeStruct((1, n_bands), F32),
            jax.ShapeDtypeStruct((n_bands, own), F32),
        ),
        in_specs=[vmem, vmem],
        out_specs=(vmem, vmem, vmem),
        name="finish",
    )(quad, proof)
    return quad, score.reshape(n_bands), proof


def solution(mesh):
    in_specs = (
        P(("grp", "dev"), None),
        P(("grp", "dev")),
        P(("grp", "dev"), None),
        P(("grp", "dev"), None),
        P(),
        P(),
    )
    out_specs = (P(), P(), P(None, ("grp", "dev")))
    return jax.shard_map(
        functools.partial(per_device, mesh.shape["grp"], mesh.shape["dev"]),
        mesh=mesh, in_specs=in_specs, out_specs=out_specs, check_vma=False
    )
```

```python
import functools
import math

import jax
import jax.numpy as jnp
from jax import lax
from jax.experimental import pallas as pl
from jax.experimental.pallas import tpu as pltpu
from jax.sharding import PartitionSpec as P

WORD_BITS = 21
CORES = 2
LOG2E = math.log2(math.e)
MESH = pl.DeviceIdType.MESH
F32 = jnp.float32
BF16 = jnp.bfloat16


def loop(count, body):
    if count == 1:
        body(0)
    else:
        lax.fori_loop(0, count, lambda i, c: (body(i), c)[1], 0)


def aligned(index, size):
    return index * size if isinstance(index, int) else pl.multiple_of(index * size, size)


def kernel(geo, samples, labels, words, corpus, grid, pick, quad_out, proof_out,
           row_s, row_c, col_s, word_in, label_in, grid_in, pick_in, row_pack, col_pack, row_vec, col_vec,
           part1, part2, part3, local_sem, rp_send, rp_recv, cp_send, cp_recv, rs_send, rs_recv,
           rc_send, rc_recv, cs_send, cs_recv, fw_send, fw_recv, p1_send, p1_recv, p2_send, p2_recv, p3_send, p3_recv):
    n_gx, n_lo, n_hi = geo
    own = samples.shape[0]
    n_bands, n_vec = quad_out.shape
    n_row, n_col, n_plane = n_gx * n_lo, n_hi * CORES, n_gx * n_lo * CORES
    rows, cols = n_row * own, n_col * own
    n_words = words.shape[1]
    total = n_row * n_col * own

    grp, dev = lax.axis_index("grp"), lax.axis_index("dev")
    gx, core = grp // CORES, grp % CORES
    z, lo = dev // n_lo, dev % n_lo
    other = 1 - core
    rslot = gx * n_lo + lo
    cslot = z * CORES + core
    pslot = rslot * CORES + core

    def at_row(slot, core_):
        return ((slot // n_lo) * CORES + core_, z * n_lo + slot % n_lo)

    def at_col(z_, core_):
        return (gx * CORES + core_, z_ * n_lo + lo)

    barrier = pltpu.get_barrier_semaphore()
    partners = []
    for t in range(1, n_plane):
        slot = (pslot + t) % n_plane
        partners.append(at_row(slot // CORES, slot % CORES))
    for t in range(1, n_hi):
        partners.append(at_col((z + t) % n_hi, core))
        partners.append(at_col((z + t) % n_hi, other))

    word_copy = pltpu.make_async_copy(words, word_in, local_sem.at[0])
    label_copy = pltpu.make_async_copy(labels, label_in, local_sem.at[1])
    word_copy.start()
    label_copy.start()
    for p in partners:
        pl.semaphore_signal(barrier, inc=1, device_id=p, device_id_type=MESH)
    own_rows = pl.ds(pl.multiple_of(rslot * own, own), own)
    own_cols = pl.ds(pl.multiple_of(cslot * own, own), own)
    keep = [
        pltpu.make_async_copy(samples, row_s.at[own_rows], local_sem.at[2]),
        pltpu.make_async_copy(corpus, row_c.at[own_rows], local_sem.at[3]),
        pltpu.make_async_copy(samples, col_s.at[own_cols], local_sem.at[4]),
        pltpu.make_async_copy(grid, grid_in, local_sem.at[5]),
        pltpu.make_async_copy(pick, pick_in, local_sem.at[6]),
    ]
    for c in keep:
        c.start()


    word_copy.wait()
    label_copy.wait()
    eye = lax.broadcasted_iota(jnp.int32, (own, own), 0) == lax.broadcasted_iota(jnp.int32, (own, own), 1)
    label_col = jnp.sum(jnp.where(eye, label_in[...].astype(F32), 0.0), axis=1, keepdims=True).astype(jnp.int32)
    groups = own // 8
    pieces = []
    width = 128 // groups
    for q in range(groups):
        pieces.append(word_in[pl.ds(8 * q, 8), :])
        pieces.append(label_col[8 * q:8 * q + 8])
        pieces.append(jnp.zeros((8, width - n_words - 1), jnp.int32))
    packed = jnp.concatenate(pieces, axis=1)
    col_pack[cslot] = packed
    row_pack[rslot] = packed

    pl.semaphore_wait(barrier, len(partners))

    def remote(src, dst, send, recv, to):
        return pltpu.make_async_remote_copy(
            src_ref=src, dst_ref=dst, send_sem=send, recv_sem=recv, device_id=to, device_id_type=MESH)

    sends = []
    col_in, fw_in, rs_in, rc_in = [], [], [], []

    def col_block(slot):
        return col_s.at[pl.ds(pl.multiple_of(slot * own, own), own)]

    def row_block(ref, slot):
        return ref.at[pl.ds(pl.multiple_of(slot * own, own), own)]

    for t in range(1, n_col):
        to = (cslot + t) % n_col
        c = remote(col_pack.at[cslot], col_pack.at[cslot], cp_send.at[t], cp_recv.at[cslot],
                   at_col(to // CORES, to % CORES))
        c.start()
        sends.append(c)
    for t in range(1, n_row):
        to = (rslot + t) % n_row
        c = remote(row_pack.at[rslot], row_pack.at[rslot], rp_send.at[t], rp_recv.at[rslot], at_row(to, core))
        c.start()
        sends.append(c)
    for t in range(1, n_hi):
        to = (z + t) % n_hi
        c = remote(samples, col_block(cslot), cs_send.at[t], cs_recv.at[z], at_col(to, core))
        c.start()
        sends.append(c)
    for t in range(1, n_row):
        to = (rslot + t) % n_row
        c = remote(samples, row_block(row_s, rslot), rs_send.at[t], rs_recv.at[rslot], at_row(to, core))
        c.start()
        sends.append(c)
    c = remote(samples, col_block(cslot), fw_send.at[z], fw_recv.at[z], at_col(z, other))
    c.start()
    sends.append(c)

    for t in range(1, n_row):
        to = (rslot + t) % n_row
        c = remote(corpus, row_block(row_c, rslot), rc_send.at[t], rc_recv.at[rslot], at_row(to, core))
        c.start()
        sends.append(c)

    for t in range(1, n_hi):
        src = (z + n_hi - t) % n_hi
        block = col_block(src * CORES + core)
        remote(samples, block, cs_send.at[t], cs_recv.at[src], at_col(src, core)).wait_recv()
        c = remote(block, block, fw_send.at[src], fw_recv.at[src], at_col(z, other))
        c.start()
        sends.append(c)

    lane = lax.broadcasted_iota(jnp.int32, (8, 128), 1)
    label_lane = lane - lane % width + n_words
    is_label = lane % width == n_words
    n_chunks = n_vec // 128
    index, mask = [], []
    for t in range(n_chunks):
        k = jnp.maximum(lane + (128 * t - 1), 0)
        w = (k * 3121) >> 16
        shift = k - w * WORD_BITS
        if t == 0:
            w = jnp.where(lane == 0, n_words, w)
            shift = jnp.where(lane == 0, 0, shift)
        index.append(w)
        mask.append(jnp.int32(1) << shift)

    def expand(tile, dst, base):
        label = jnp.take_along_axis(tile, label_lane, axis=1)
        tile = jnp.where(is_label, label ^ 1, tile ^ (0 - label))
        for t in range(n_chunks):
            parts = []
            for q in range(groups):
                got = jnp.take_along_axis(tile, index[t] + q * width, axis=1)
                parts.append(jnp.where((got & mask[t]) != 0, 1.0, -1.0).astype(F32))
            dst[pl.ds(base, own), pl.ds(128 * t, 128)] = jnp.concatenate(parts, axis=0).astype(dst.dtype)

    for t in range(1, n_col):
        src = (cslot + n_col - t) % n_col
        remote(col_pack.at[src], col_pack.at[src], cp_send.at[t], cp_recv.at[src],
               at_col(src // CORES, src % CORES)).wait_recv()
    for t in range(1, n_row):
        src = (rslot + n_row - t) % n_row
        remote(row_pack.at[src], row_pack.at[src], rp_send.at[t], rp_recv.at[src], at_row(src, core)).wait_recv()
    for slot in range(n_col):
        expand(col_pack[slot], col_vec, slot * own)
    for slot in range(n_row):
        expand(row_pack[slot], row_vec, slot * own)

    for c in keep:
        c.wait()
    for t in range(n_hi):
        src = (z + n_hi - t) % n_hi
        block = col_block(src * CORES + other)
        remote(samples, block, fw_send.at[src], fw_recv.at[src], at_col(z, other)).wait_recv()
    for t in range(1, n_row):
        src = (rslot + n_row - t) % n_row
        remote(samples, row_block(row_s, src), rs_send.at[t], rs_recv.at[src], at_row(src, core)).wait_recv()

    rb, cb = min(128, rows), min(256, cols)
    gains = [jnp.full((1, 1), -0.5 * LOG2E, F32) / jnp.full((1, 1), grid_in[pick_in[b]], F32) for b in range(n_bands)]
    diag = lax.broadcasted_iota(jnp.int32, (cb, cb), 0) == lax.broadcasted_iota(jnp.int32, (cb, cb), 1)
    if rows > rb or cols > cb:
        part1[pslot] = jnp.zeros(part1.shape[1:], F32)
        part3[rslot] = jnp.zeros(part3.shape[1:], F32)

    def squares(x):
        wide = x.astype(F32)
        return jnp.sum(wide * wide, axis=1, keepdims=True)

    def kerns(left, right, right_sq):
        cross = lax.dot_general(left, right, (((1,), (1,)), ((), ())), preferred_element_type=F32)
        dist = squares(left) + right_sq - 2.0 * cross
        return jnp.concatenate([jnp.exp2(dist * g).astype(BF16) for g in gains], axis=0)

    def add_to(ref, slot, lanes, value):
        if rows > rb or cols > cb:
            value = ref[slot, :, lanes] + value
        ref[slot, :, lanes] = value

    def columns(cc):
        here = pl.ds(aligned(cc, cb), cb)
        right = col_s[here, :]
        return here, right, jnp.sum(jnp.where(diag, squares(right), 0.0), axis=0, keepdims=True)

    def test_chunk(cc):
        here, right, right_sq = columns(cc)
        vec = col_vec[here, :]

        def row_chunk(rc):
            there = pl.ds(aligned(rc, rb), rb)
            kern = kerns(row_s[there, :], right, right_sq)
            prod = jnp.dot(kern, vec, preferred_element_type=F32)
            mine = row_vec[there, :]
            forms = [jnp.sum(mine * prod[b * rb:(b + 1) * rb], axis=0, keepdims=True) for b in range(n_bands)]
            add_to(part1, pslot, pl.ds(0, n_vec), jnp.concatenate(forms, axis=0))

        loop(rows // rb, row_chunk)

    def proof_chunk(cc):
        here, right, right_sq = columns(cc)
        vec = col_vec[here, :128]

        def row_chunk(rc):
            there = pl.ds(aligned(rc, rb), rb)
            kern = kerns(row_c[there, :], right, right_sq)
            flat = lax.dot_general(vec, kern, (((0,), (1,)), ((), ())), preferred_element_type=F32)
            proof = jnp.concatenate([flat[0:1, b * rb:(b + 1) * rb] for b in range(n_bands)], axis=0)
            add_to(part3, rslot, there, proof)

        loop(rows // rb, row_chunk)

    loop(cols // cb, test_chunk)

    for t in range(1, n_plane):
        to = (pslot + t) % n_plane
        c = remote(part1.at[pslot], part1.at[pslot], p1_send.at[t], p1_recv.at[pslot],
                   at_row(to // CORES, to % CORES))
        c.start()
        sends.append(c)
    for t in range(1, n_row):
        src = (rslot + n_row - t) % n_row
        remote(corpus, row_block(row_c, src), rc_send.at[t], rc_recv.at[src], at_row(src, core)).wait_recv()
    loop(cols // cb, proof_chunk)
    for t in range(1, n_row):
        to = (rslot + t) % n_row
        c = remote(part3.at[rslot], part3.at[rslot], p3_send.at[t], p3_recv.at[rslot], at_row(to, core))
        c.start()
        sends.append(c)
    for t in range(1, n_plane):
        src = (pslot + n_plane - t) % n_plane
        remote(part1.at[src], part1.at[src], p1_send.at[t], p1_recv.at[src],
               at_row(src // CORES, src % CORES)).wait_recv()
    quad = part1[0]
    for slot in range(1, n_plane):
        quad = quad + part1[slot]
    part2[z] = quad
    for t in range(1, n_hi):
        to = (z + t) % n_hi
        c = remote(part2.at[z], part2.at[z], p2_send.at[t], p2_recv.at[z], at_col(to, core))
        c.start()
        sends.append(c)
    for t in range(1, n_row):
        src = (rslot + n_row - t) % n_row
        remote(part3.at[src], part3.at[src], p3_send.at[t], p3_recv.at[src], at_row(src, core)).wait_recv()
    proof = part3[0]
    for slot in range(1, n_row):
        proof = proof + part3[slot]
    mine = jnp.zeros((n_bands, own), F32)
    for slot in range(n_row):
        mine = jnp.where(rslot == slot, proof[:, slot * own:(slot + 1) * own], mine)
    proof_out[...] = mine * F32(1.0 / math.sqrt(total))
    for t in range(1, n_hi):
        src = (z + n_hi - t) % n_hi
        remote(part2.at[src], part2.at[src], p2_send.at[t], p2_recv.at[src], at_col(src, core)).wait_recv()
    quad = part2[0]
    for slot in range(1, n_hi):
        quad = quad + part2[slot]
    quad = quad * F32(1.0 / total)
    quad_out[...] = quad
    for c in sends:
        c.wait_send()


def finish(quad_in, proof_in, quad_out, score_out, proof_out):
    quad = quad_in[...]
    quad_out[...] = quad
    proof_out[...] = proof_in[...]
    n_bands, n_vec = quad.shape
    boot = lax.broadcasted_iota(jnp.int32, quad.shape, 1) > 0
    count = F32(1.0 / (n_vec - 1))
    centre = jnp.sum(jnp.where(boot, quad, 0.0), axis=1, keepdims=True) * count
    off = quad - centre
    spread = jnp.sum(jnp.where(boot, off * off, 0.0), axis=1, keepdims=True) * count
    score = (quad[:, :1] - centre) / jnp.sqrt(spread + 1e-6)
    spot = lax.broadcasted_iota(jnp.int32, (n_bands, n_bands), 0) == lax.broadcasted_iota(
        jnp.int32, (n_bands, n_bands), 1)
    score_out[...] = jnp.sum(jnp.where(spot, score, 0.0), axis=0, keepdims=True)


def per_device(n_grp, n_dev, samples, labels, words, corpus, grid, pick):
    n_lo = 2 if n_dev % 2 == 0 else 1
    n_gx, n_hi = n_grp // CORES, n_dev // n_lo
    n_row, n_col, n_plane = n_gx * n_lo, n_hi * CORES, n_gx * n_lo * CORES
    own, width = samples.shape
    rows, cols = n_row * own, n_col * own
    n_bands, n_vec = pick.shape[0], 512
    dma = lambda n: pltpu.SemaphoreType.DMA((n,))
    any_ = pl.BlockSpec(memory_space=pl.ANY)
    vmem = pl.BlockSpec(memory_space=pltpu.VMEM)
    quad, proof = pl.pallas_call(
        functools.partial(kernel, (n_gx, n_lo, n_hi)),
        out_shape=(
            jax.ShapeDtypeStruct((n_bands, n_vec), F32),
            jax.ShapeDtypeStruct((n_bands, own), F32),
        ),
        in_specs=[any_] * 6,
        out_specs=(vmem, vmem),
        scratch_shapes=[
            pltpu.VMEM((rows, width), BF16),
            pltpu.VMEM((rows, width), BF16),
            pltpu.VMEM((cols, width), BF16),
            pltpu.VMEM(words.shape, jnp.int32),
            pltpu.VMEM((1, own), jnp.int32),
            pltpu.SMEM(grid.shape, F32),
            pltpu.SMEM(pick.shape, jnp.int32),
            pltpu.VMEM((n_row, 8, 128), jnp.int32),
            pltpu.VMEM((n_col, 8, 128), jnp.int32),
            pltpu.VMEM((rows, n_vec), F32),
            pltpu.VMEM((cols, n_vec), BF16),
            pltpu.VMEM((n_plane, n_bands, n_vec), F32),
            pltpu.VMEM((n_hi, n_bands, n_vec), F32),
            pltpu.VMEM((n_row, n_bands, rows), F32),
            dma(7),
            dma(n_row), dma(n_row), dma(n_col), dma(n_col), dma(n_row), dma(n_row),
            dma(n_row), dma(n_row), dma(n_hi), dma(n_hi), dma(n_hi), dma(n_hi),
            dma(n_plane), dma(n_plane), dma(n_hi), dma(n_hi), dma(n_row), dma(n_row),
        ],
        compiler_params=pltpu.CompilerParams(
            collective_id=0, has_side_effects=True, vmem_limit_bytes=62 * 1024 * 1024),
        name="two_sample",
    )(samples, labels.reshape(1, own), words, corpus, grid, pick)
    quad, score, proof = pl.pallas_call(
        finish,
        out_shape=(
            jax.ShapeDtypeStruct((n_bands, n_vec), F32),
            jax.ShapeDtypeStruct((1, n_bands), F32),
            jax.ShapeDtypeStruct((n_bands, own), F32),
        ),
        in_specs=[vmem, vmem],
        out_specs=(vmem, vmem, vmem),
        name="finish",
    )(quad, proof)
    return quad, score.reshape(n_bands), proof


def solution(mesh):
    in_specs = (
        P(("grp", "dev"), None),
        P(("grp", "dev")),
        P(("grp", "dev"), None),
        P(("grp", "dev"), None),
        P(),
        P(),
    )
    out_specs = (P(), P(), P(None, ("grp", "dev")))
    return jax.shard_map(
        functools.partial(per_device, mesh.shape["grp"], mesh.shape["dev"]),
        mesh=mesh, in_specs=in_specs, out_specs=out_specs, check_vma=False
    )
```
